256 devices in a mesh: grp: 64 (over x, z_hi, y), tp: 4 (over z_lo, core).
Axes of the slice: x: 4, y: 4, z: 8 (z_hi: 4, z_lo: 2; z = z_hi * 2 + z_lo), core: 2. Of those that a mesh axis runs over, the one named last changes fastest.
Arguments:
- queries: bfloat16 [4, 128, 8192], P(None, 'grp')
- new_keys: bfloat16 [4, 128, 1024], P(None, 'grp'), may hold values from -6 to 6
- new_values: bfloat16 [4, 128, 1024], P(None, 'grp'), may hold values from -6 to 6
- key_cache: bfloat16 [64, 4, 6, 64, 1024], P('grp', 'tp'), may hold values from -6 to 6
- value_cache: bfloat16 [64, 4, 6, 64, 1024], P('grp', 'tp'), may hold values from -6 to 6
- page_table: int32 [128, 12], P('grp'), may hold values from 0 to 5, as said below
- context: int32 [128], P('grp'), may hold values from 1 to 764
- light_q: bfloat16 [4, 128, 8192], P(None, 'grp', 'tp'), may hold values from -6 to 6
- light_k: bfloat16 [4, 128, 8192], P(None, 'grp', 'tp'), may hold values from -0.5 to 0.5
- light_v: bfloat16 [4, 128, 8192], P(None, 'grp', 'tp'), may hold values from -6 to 6
- light_state: float32 [128, 64, 128, 128], P('grp', 'tp'), may hold values from -0.6 to 0.6
- decay_rate: float32 [64], P('tp'), may hold values from 0.01 to 1
- move_dist: int32 [2], replicated, may hold values from 1 to 63
- move_slot: int32 [2], replicated, may hold values from 0 to 1, as said below
Outputs:
- soft_mix: bfloat16 [4, 128, 8192], P(None, 'grp', 'tp')
- linear_mix: bfloat16 [4, 128, 8192], P(None, 'grp', 'tp')
- key_pages: bfloat16 [64, 4, 6, 64, 1024], P('grp', 'tp')
- value_pages: bfloat16 [64, 4, 6, 64, 1024], P('grp', 'tp')
- linear_states: float32 [128, 64, 128, 128], P('grp', 'tp')
- moved_table: int32 [128, 12], P('grp')
- moved_lengths: int32 [128], P('grp')
The draws below stay inside these ranges and needn't reach their ends.
Inputs may be any that keep to these rules, and one draw needn't show every extreme that they name: `page_table`: slot i of a group owns pages i * 3 to i * 3 + 2 of each part; the row of a request lists, for each part, each of its pages once. `move_slot`: the sections name distinct slots.
All inputs are finite; a program needn't handle non-finite values.
Results may differ from the reference program's by a relative error of at most 0.017.
Values may be sent and summed in bfloat16 or wider, within the bound.
No kernel may reach another device: no remote copies, remote signals or barrier semaphores. Data moves between devices by JAX's collectives and lax.ppermute only.
A program may use at most 128 MiB of HBM per device.

```python
import math
import jax
import jax.numpy as jnp
from jax import lax

HEADS = 64
KV_HEADS = 8
HEAD_DIM = 128
R_DEV = 2
PR = 3
PAGE = 64
STEPS = 4
SECTIONS = 2
KVW = 1024
POOL = 6
MAXP = 12
REQUESTS = 128
N_GRP = 64
N_TP = 4


def draw_queries(key, part):
    key = jax.random.fold_in(key, 37)
    first_key = jax.random.fold_in(key, 0)
    base = jax.random.normal(first_key, (STEPS, REQUESTS, HEADS, HEAD_DIM), jnp.float32)
    return base.reshape(STEPS, REQUESTS, HEADS * HEAD_DIM).astype(jnp.bfloat16)


def draw_page_table(key, part):
    key = jax.random.fold_in(key, 11)
    ranking = jax.random.randint(key, (REQUESTS, N_TP, PR), 0, 1 << 20)
    ranking = ranking * PR + jnp.arange(PR, dtype=jnp.int32)
    order = jnp.argsort(ranking, axis=2, stable=True).astype(jnp.int32)
    offsets = jnp.arange(REQUESTS, dtype=jnp.int32) % R_DEV * PR
    local = order + offsets[:, None, None]
    return jnp.transpose(local, (0, 2, 1)).reshape(REQUESTS, MAXP)


def draw_context(key, part):
    key = jax.random.fold_in(key, 23)
    first_key, second_key = jax.random.split(key)
    longest = MAXP * PAGE - STEPS
    lengths = jax.random.randint(first_key, (REQUESTS,), 1, longest + 1)
    chosen = jax.random.randint(second_key, (), 0, REQUESTS)
    return jnp.where(jnp.arange(REQUESTS) == chosen, longest, lengths).astype(jnp.int32)


def draw_move_slot(key, part):
    key = jax.random.fold_in(key, 41)
    shuffled = jax.random.permutation(key, jnp.arange(R_DEV, dtype=jnp.int32))
    return shuffled[:SECTIONS].astype(jnp.int32)


def block_scale(key, shape, pieces, low, largest):
    gain, own = 1.0, jax.random.fold_in(key, 6)
    for axis_at, blocks in pieces:
        heights = jnp.exp(jax.random.uniform(jax.random.fold_in(own, axis_at), (blocks,), jnp.float32, low / len(pieces), largest / len(pieces)))
        gain = gain * jnp.repeat(heights, shape[axis_at] // blocks).reshape([-1 if axis == axis_at else 1 for axis in range(len(shape))])
    return gain


def gaussian(stream_key, shape, scale, bound, cuts=(), kind=jnp.bfloat16):
    values = scale * jax.random.normal(stream_key, shape, jnp.float32)
    if cuts:
        values = values * block_scale(stream_key, shape, cuts, -0.22, 0.18)
    return jnp.clip(values, -bound, bound).astype(kind)


def setup_inputs(seed: int = 0) -> dict:
    seeds = jax.random.split(jax.random.key(seed), 15)
    queries = draw_queries(jax.random.fold_in(seeds[14], 71), 0)
    new_keys = gaussian(seeds[1], (STEPS, REQUESTS, KVW), 1.0, 6.0, ((1, 64),))
    new_values = gaussian(seeds[2], (STEPS, REQUESTS, KVW), 1.0, 6.0, ((1, 64),))
    key_cache = gaussian(seeds[3], (N_GRP, N_TP, POOL, PAGE, KVW), 1.0, 6.0, ((0, 64), (1, 4)))
    value_cache = gaussian(seeds[4], (N_GRP, N_TP, POOL, PAGE, KVW), 1.0, 6.0, ((0, 64), (1, 4)))
    page_table = draw_page_table(jax.random.fold_in(seeds[14], 71), 0)
    context = draw_context(jax.random.fold_in(seeds[14], 71), 0)
    light_q = gaussian(seeds[7], (STEPS, REQUESTS, HEADS * HEAD_DIM), 1.0, 6.0, ((1, 64), (2, 4)))
    light_k = gaussian(seeds[8], (STEPS, REQUESTS, HEADS * HEAD_DIM), 0.088, 0.5, ((1, 64), (2, 4)))
    light_v = gaussian(seeds[9], (STEPS, REQUESTS, HEADS * HEAD_DIM), 1.0, 6.0, ((1, 64), (2, 4)))
    light_state = gaussian(seeds[10], (REQUESTS, HEADS, HEAD_DIM, HEAD_DIM), 0.088, 0.6, ((0, 64), (1, 4)), jnp.float32)
    decay_rate = jnp.clip(jnp.exp(math.log(1.0) - 4.6051702 * jax.random.uniform(seeds[11], (HEADS,), jnp.float32) ** block_scale(seeds[11], (HEADS,), ((0, 4),), -0.2, 0.2)), 0.01, 1.0)
    move_dist = jax.random.randint(seeds[12], (SECTIONS,), 1, N_GRP).astype(jnp.int32)
    move_slot = draw_move_slot(jax.random.fold_in(seeds[14], 71), 0)
    return dict(queries=queries, new_keys=new_keys, new_values=new_values, key_cache=key_cache, value_cache=value_cache, page_table=page_table, context=context, light_q=light_q, light_k=light_k, light_v=light_v, light_state=light_state, decay_rate=decay_rate, move_dist=move_dist, move_slot=move_slot)


MASKED_SCORE = -1.0e30


def write_pool(kv_pool, page_rows, lengths, new_rows):
    places = lengths[:, None] + jnp.arange(STEPS, dtype=jnp.int32)[None, :]
    logical = places // PAGE
    owner = logical % N_TP
    page_index = jnp.take_along_axis(page_rows, logical, axis=1)
    return kv_pool.at[owner, page_index, places % PAGE].set(new_rows)


def group_attend(packed):
    group_keys, group_values, page_rows, lengths, group_queries, fresh_keys, fresh_values = packed
    group_keys = write_pool(group_keys, page_rows, lengths, jnp.swapaxes(fresh_keys, 0, 1))
    group_values = write_pool(group_values, page_rows, lengths, jnp.swapaxes(fresh_values, 0, 1))
    logical = jnp.arange(MAXP, dtype=jnp.int32)
    seq_keys = group_keys[(logical % N_TP)[None, :], page_rows]
    seq_values = group_values[(logical % N_TP)[None, :], page_rows]
    seq_keys = seq_keys.reshape(R_DEV, MAXP * PAGE, KV_HEADS, HEAD_DIM).astype(jnp.float32)
    seq_values = seq_values.reshape(R_DEV, MAXP * PAGE, KV_HEADS, HEAD_DIM).astype(jnp.float32)
    grouped = group_queries.reshape(STEPS, R_DEV, KV_HEADS, HEADS // KV_HEADS, HEAD_DIM).astype(jnp.float32)
    scores = jnp.einsum("srkgd,rlkd->srkgl", grouped, seq_keys) * HEAD_DIM ** -0.5
    places = jnp.arange(MAXP * PAGE, dtype=jnp.int32)
    last_place = lengths[None, :] + jnp.arange(STEPS, dtype=jnp.int32)[:, None]
    visible = (places[None, None, :] <= last_place[:, :, None])[:, :, None, None, :]
    row_top = jnp.max(jnp.where(visible, scores, MASKED_SCORE), axis=-1, keepdims=True)
    weights = jnp.where(visible, jnp.exp(scores - row_top), 0.0)
    row_total = jnp.sum(weights, axis=-1)
    mixed = jnp.einsum("srkgl,rlkd->srkgd", weights.astype(jnp.bfloat16).astype(jnp.float32), seq_values)
    output = (mixed / row_total[..., None]).reshape(STEPS, R_DEV, HEADS * HEAD_DIM).astype(jnp.bfloat16)
    return group_keys, group_values, output


def by_group(array):
    shape = array.shape
    return jnp.swapaxes(array.reshape((shape[0], N_GRP, R_DEV) + shape[2:]), 0, 1)


def move_slot_of(whole, slot_index, distance):
    moved = jnp.roll(whole[:, slot_index], distance, axis=0)
    return whole.at[:, slot_index].set(moved)


def reference(queries, new_keys, new_values, key_cache, value_cache, page_table, context, light_q, light_k, light_v, light_state, decay_rate, move_dist, move_slot):
    tables = page_table.reshape(N_GRP, R_DEV, MAXP)
    lengths = context.reshape(N_GRP, R_DEV)
    written_keys, written_values, soft_groups = lax.map(group_attend, (key_cache, value_cache, tables, lengths, by_group(queries), by_group(new_keys), by_group(new_values)))
    soft_mix = jnp.swapaxes(soft_groups, 0, 1).reshape(STEPS, REQUESTS, HEADS * HEAD_DIM)
    lin_state = light_state
    fading = jnp.exp(-decay_rate)[None, :, None, None]
    outputs = []
    for step_no in range(STEPS):
        query_now = light_q[step_no].reshape(REQUESTS, HEADS, HEAD_DIM).astype(jnp.float32)
        key_now = light_k[step_no].reshape(REQUESTS, HEADS, HEAD_DIM).astype(jnp.float32)
        value_now = light_v[step_no].reshape(REQUESTS, HEADS, HEAD_DIM).astype(jnp.float32)
        lin_state = fading * lin_state + key_now[..., :, None] * value_now[..., None, :]
        outputs.append(jnp.einsum("rhd,rhde->rhe", query_now, lin_state, precision=lax.Precision.HIGHEST).reshape(REQUESTS, HEADS * HEAD_DIM))
    linear_mix = jnp.stack(outputs).astype(jnp.bfloat16)
    key_slots = jnp.swapaxes(written_keys.reshape(N_GRP, N_TP, R_DEV, PR, PAGE, KVW), 1, 2)
    value_slots = jnp.swapaxes(written_values.reshape(N_GRP, N_TP, R_DEV, PR, PAGE, KVW), 1, 2)
    state_slots = lin_state.reshape(N_GRP, R_DEV, HEADS, HEAD_DIM, HEAD_DIM)
    for section_no in range(SECTIONS):
        slot_index = move_slot[section_no]
        distance = move_dist[section_no]
        key_slots = move_slot_of(key_slots, slot_index, distance)
        value_slots = move_slot_of(value_slots, slot_index, distance)
        state_slots = move_slot_of(state_slots, slot_index, distance)
        tables = move_slot_of(tables, slot_index, distance)
        lengths = move_slot_of(lengths, slot_index, distance)
    key_pages = jnp.swapaxes(key_slots, 1, 2).reshape(N_GRP, N_TP, POOL, PAGE, KVW)
    value_pages = jnp.swapaxes(value_slots, 1, 2).reshape(N_GRP, N_TP, POOL, PAGE, KVW)
    linear_states = state_slots.reshape(REQUESTS, HEADS, HEAD_DIM, HEAD_DIM)
    moved_table = tables.reshape(REQUESTS, MAXP)
    moved_lengths = (lengths.reshape(REQUESTS) + STEPS).astype(jnp.int32)
    return soft_mix, linear_mix, key_pages, value_pages, linear_states, moved_table, moved_lengths
```

```python
import functools

import jax
import jax.numpy as jnp
from jax import lax
from jax.experimental import pallas as pl
from jax.experimental.pallas import tpu as pltpu
from jax.sharding import PartitionSpec as P

MASKED_SCORE = -1e30
LANES = 128
META_ROWS = 16
VMEM_BYTES = 48 * 1024 * 1024
DIMS0 = (((0,), (0,)), ((), ()))
DIMS1 = (((1,), (1,)), ((), ()))


def whole():
    return pl.BlockSpec(memory_space=pltpu.VMEM)


def scalars():
    return pl.BlockSpec(memory_space=pltpu.SMEM)


def cost(flops, moved, exps=0):
    return pl.CostEstimate(flops=flops, bytes_accessed=moved, transcendentals=exps)


def joined_rows(ref):
    value = ref[...].astype(jnp.float32)
    return jnp.concatenate([value[step] for step in range(value.shape[0])], axis=0)


def pack_kernel(
    table, context, decay, new_keys, new_values, key_cache, value_cache, light_q, light_k, light_v,
    state, pack_0, pack_1, linear_mix, rows_q, rows_k, rows_v, rows_out,
):
    steps, slots, width = new_keys.shape
    page_len = key_cache.shape[3]
    per_slot = key_cache.shape[2] // slots
    heads = state.shape[1]
    kv_rows = per_slot * page_len
    tp_rank, tp_count = lax.axis_index("tp"), lax.axis_size("tp")
    packs = (pack_0, pack_1)
    across = width // LANES
    state_rows = heads // across * LANES

    for slot in range(slots):
        pack = packs[slot]
        for page in range(per_slot):
            at = page * page_len
            pack[at : at + page_len, :] = key_cache[0, 0, slot * per_slot + page]
            pack[kv_rows + at : kv_rows + at + page_len, :] = value_cache[0, 0, slot * per_slot + page]
        for step in range(steps):
            place = context[slot] + step
            logical = place // page_len

            @pl.when(logical % tp_count == tp_rank)
            def _():
                row = (table[slot, logical] - slot * per_slot) * page_len + place % page_len
                base = pl.multiple_of(row // 16 * 16, 16)
                hit = lax.broadcasted_iota(jnp.int32, (16, width), 0) == row - base
                for fresh, first in ((new_keys, 0), (new_values, kv_rows)):
                    line = fresh[step].astype(jnp.float32)[slot : slot + 1]
                    here = pl.ds(pl.multiple_of(first + base, 16), 16)
                    old = pack[here, :].astype(jnp.float32)
                    pack[here, :] = jnp.where(hit, line, old).astype(jnp.bfloat16)

        lane = lax.broadcasted_iota(jnp.int32, (META_ROWS, width), 1)
        meta = jnp.zeros((META_ROWS, width), jnp.float32)
        entries = [table[slot, logical] for logical in range(table.shape[1])]
        entries += [context[slot] // 256, context[slot] % 256]
        for index, entry in enumerate(entries):
            meta = jnp.where(lane == index, entry.astype(jnp.float32), meta)
        pack[2 * kv_rows + state_rows :, :] = meta.astype(jnp.bfloat16)

    rows_q[...] = joined_rows(light_q)
    rows_k[...] = joined_rows(light_k)
    rows_v[...] = joined_rows(light_v)
    rows = steps * slots
    row = lax.broadcasted_iota(jnp.int32, (rows, LANES), 0)
    step_of = (row // slots).astype(jnp.float32)
    first = row % slots == 0
    pair_row = lax.broadcasted_iota(jnp.int32, (rows, rows), 0)
    pair_col = lax.broadcasted_iota(jnp.int32, (rows, rows), 1)
    gap = pair_row // slots - pair_col // slots
    counted = (pair_row % slots == pair_col % slots) & (gap >= 0)
    gap = jnp.maximum(gap, 0).astype(jnp.float32)
    for head in range(heads):
        lanes = slice(head * LANES, (head + 1) * LANES)
        rate = decay[head]
        query, key, value = rows_q[:, lanes], rows_k[:, lanes], rows_v[:, lanes]
        q16, k16, v16 = (part.astype(jnp.bfloat16) for part in (query, key, value))
        aged = key * jnp.exp((step_of - (steps - 1)) * rate)
        aged = jnp.concatenate([jnp.where(first, aged, 0.0), jnp.where(first, 0.0, aged)], axis=1)
        added = lax.dot_general(
            aged.astype(jnp.bfloat16), v16, DIMS0, preferred_element_type=jnp.float32
        )
        fade = jnp.exp(jnp.full((1, LANES), -float(steps), jnp.float32) * rate)
        start = [state[slot, head] for slot in range(slots)]
        at = 2 * kv_rows + head // across * LANES
        over = slice(head % across * LANES, (head % across + 1) * LANES)
        for slot in range(slots):
            final = start[slot] * fade + added[slot * LANES : (slot + 1) * LANES]
            packs[slot][at : at + LANES, over] = final.astype(jnp.bfloat16)
        both = jnp.concatenate([part.astype(jnp.bfloat16) for part in start], axis=1)
        base = jnp.dot(q16, both, preferred_element_type=jnp.float32)
        base = jnp.where(first, base[:, :LANES], base[:, LANES:])
        base = base * jnp.exp(-(step_of + 1.0) * rate)
        match = lax.dot_general(q16, k16, DIMS1, preferred_element_type=jnp.float32)
        match = jnp.where(counted, match * jnp.exp(-gap * rate), 0.0)
        recent = jnp.dot(match.astype(jnp.bfloat16), v16, preferred_element_type=jnp.float32)
        rows_out[:, lanes] = base + recent
    for step in range(steps):
        linear_mix[step] = rows_out[step * slots : (step + 1) * slots, :].astype(jnp.bfloat16)


def thirds(value):
    high = value.astype(jnp.bfloat16)
    rest = value - high.astype(jnp.float32)
    middle = rest.astype(jnp.bfloat16)
    low = (rest - middle.astype(jnp.float32)).astype(jnp.bfloat16)
    return [part.astype(jnp.float32) for part in (high, middle, low)]


def attend_kernel(page_len, table, context, queries, pack_0, pack_1, *rest):
    sends, rows_q = rest[:-1], rest[-1]
    steps, slots, _ = queries.shape
    tp_rank, tp_count = lax.axis_index("tp"), lax.axis_size("tp")
    kv_rows = pack_0.shape[0] // 2
    per_slot = kv_rows // page_len
    width = pack_0.shape[1]
    kv_heads = width // LANES
    share = queries.shape[2] // LANES // kv_heads
    rows = steps * slots
    packs = (pack_0, pack_1)
    rows_q[...] = joined_rows(queries)
    count = share * rows
    row = lax.broadcasted_iota(jnp.int32, (count, kv_rows), 0) % rows
    column = lax.broadcasted_iota(jnp.int32, (count, kv_rows), 1)
    limits = []
    for slot in range(slots):
        base = jnp.zeros((count, kv_rows), jnp.int32)
        for page in range(per_slot):
            number = slot * per_slot + page
            logical = 0
            for turn in range(per_slot):
                guess = turn * tp_count + tp_rank
                logical = logical + jnp.where(table[slot, guess] == number, guess, 0)
            base = jnp.where(column // page_len == page, logical * page_len, base)
        limits.append(context[slot] + row // slots - base - column % page_len)
    first = row % slots == 0
    visible = jnp.where(first, limits[0], limits[1]) >= 0
    first_out = first[:, :LANES]
    lane = lax.broadcasted_iota(jnp.int32, (count, LANES), 1)
    scale = float(LANES) ** -0.5
    per_part = kv_heads // tp_count
    for turn in range(tp_count):
        target = jnp.bitwise_xor(tp_rank, turn)
        for half in range(per_part):
            head = target * per_part + half
            over = pl.ds(pl.multiple_of(head * LANES, LANES), LANES)
            query = jnp.concatenate(
                [
                    rows_q[:, pl.ds(pl.multiple_of((head * share + one) * LANES, LANES), LANES)]
                    for one in range(share)
                ],
                axis=0,
            ).astype(jnp.bfloat16)
            scores = [
                lax.dot_general(
                    query, pack[:kv_rows, over], DIMS1, preferred_element_type=jnp.float32
                )
                for pack in packs
            ]
            scores = jnp.where(visible, jnp.where(first, *scores) * scale, MASKED_SCORE)
            top = jnp.max(scores, axis=-1, keepdims=True)
            weights = jnp.where(visible, jnp.exp(scores - top), 0.0)
            total = jnp.sum(weights, axis=-1, keepdims=True)
            weights = weights.astype(jnp.bfloat16)
            mixed = [
                jnp.dot(weights, pack[kv_rows:, over], preferred_element_type=jnp.float32)
                for pack in packs
            ]
            at = slice(half * count, (half + 1) * count)
            sends[turn][at, :LANES] = jnp.where(first_out, *mixed).astype(jnp.bfloat16)
            extra = jnp.zeros((count, LANES), jnp.float32)
            for index, part in enumerate(thirds(top) + thirds(total)):
                extra = jnp.where(lane == index, part, extra)
            sends[turn][at, LANES:] = extra.astype(jnp.bfloat16)


def merge_kernel(*refs):
    parts, soft_mix, rows_out = refs[:-2], refs[-2], refs[-1]
    steps, slots, width = soft_mix.shape
    rows = steps * slots
    tops, totals = [], []
    for part in parts:
        extra = part[:, LANES:].astype(jnp.float32)
        tops.append(extra[:, 0:1] + extra[:, 1:2] + extra[:, 2:3])
        totals.append(extra[:, 3:4] + extra[:, 4:5] + extra[:, 5:6])
    peak = functools.reduce(jnp.maximum, tops)
    scales = [jnp.exp(top - peak) for top in tops]
    total = sum(total * scale for total, scale in zip(totals, scales))
    mixed = sum(part[:, :LANES].astype(jnp.float32) * scale for part, scale in zip(parts, scales))
    mixed = mixed / total
    for one in range(width // LANES):
        rows_out[:, one * LANES : (one + 1) * LANES] = mixed[one * rows : (one + 1) * rows]
    for step in range(steps):
        soft_mix[step] = rows_out[step * slots : (step + 1) * slots, :].astype(jnp.bfloat16)


def unpack_kernel(steps, landed_0, landed_1, keys, values, states, table, lengths):
    slots, heads = states.shape[:2]
    page_len, width = keys.shape[3:]
    per_slot = keys.shape[2] // slots
    kv_rows = per_slot * page_len
    across = width // LANES
    state_rows = heads // across * LANES
    entries = table.shape[1]
    for slot, landed in enumerate((landed_0, landed_1)):
        for page in range(per_slot):
            at = page * page_len
            keys[0, 0, slot * per_slot + page] = landed[at : at + page_len, :]
            values[0, 0, slot * per_slot + page] = landed[kv_rows + at : kv_rows + at + page_len, :]
        for head in range(heads):
            at = 2 * kv_rows + head // across * LANES
            over = slice(head % across * LANES, (head % across + 1) * LANES)
            states[slot, head] = landed[at : at + LANES, over].astype(jnp.float32)
        meta = landed[2 * kv_rows + state_rows :, :LANES].astype(jnp.float32)[:1]
        table[slot : slot + 1, :] = meta[:, :entries].astype(jnp.int32)
        lane = lax.broadcasted_iota(jnp.int32, meta.shape, 1)
        weight = jnp.where(lane == entries, 256.0, jnp.where(lane == entries + 1, 1.0, 0.0))
        lengths[slot] = jnp.sum(meta * weight).astype(jnp.int32) + steps


def moved(value, distance):
    count = lax.axis_size("grp")
    return lax.ppermute(value, "grp", [(at, (at + distance) % count) for at in range(count)])


def migrated(value, distance):
    count = lax.axis_size("grp")
    routes = [functools.partial(moved, distance=step) for step in range(1, count)]
    return lax.switch(distance - 1, routes, value)


def per_device(
    queries,
    new_keys,
    new_values,
    key_cache,
    value_cache,
    page_table,
    context,
    light_q,
    light_k,
    light_v,
    light_state,
    decay_rate,
    move_dist,
    move_slot,
):
    steps, slots, width = new_keys.shape
    page_len = key_cache.shape[3]
    heads = light_state.shape[1]
    kv_rows = key_cache.shape[2] // slots * page_len
    pack_rows = 2 * kv_rows + heads * LANES * LANES // width + META_ROWS
    tp_count = lax.axis_size("tp")
    rows = steps * slots
    params = pltpu.CompilerParams(vmem_limit_bytes=VMEM_BYTES)
    pack_shape = jax.ShapeDtypeStruct((pack_rows, width), jnp.bfloat16)
    line = pltpu.VMEM((rows, heads * LANES), jnp.float32)

    pack_0, pack_1, linear_mix = pl.pallas_call(
        pack_kernel,
        out_shape=(pack_shape, pack_shape, jax.ShapeDtypeStruct(light_q.shape, jnp.bfloat16)),
        in_specs=[scalars()] * 3 + [whole()] * 8,
        out_specs=(whole(), whole(), whole()),
        scratch_shapes=[line] * 4,
        compiler_params=params,
        cost_estimate=cost(1 << 24, 7 << 20),
        name="pack",
    )(
        page_table, context, decay_rate, new_keys, new_values, key_cache, value_cache,
        light_q, light_k, light_v, light_state,
    )

    send_rows = rows * queries.shape[2] // LANES // tp_count
    send_shape = jax.ShapeDtypeStruct((send_rows, 2 * LANES), jnp.bfloat16)
    sends = pl.pallas_call(
        functools.partial(attend_kernel, page_len),
        grid=(1,),
        out_shape=(send_shape,) * tp_count,
        in_specs=[scalars()] * 2
        + [whole()]
        + [pl.BlockSpec((2 * kv_rows, width), lambda i: (0, 0))] * 2,
        out_specs=(whole(),) * tp_count,
        scratch_shapes=[pltpu.VMEM((rows, queries.shape[2]), jnp.float32)],
        compiler_params=params,
        cost_estimate=cost(1 << 28, 2 << 20, 1 << 18),
        name="attend",
    )(page_table, context, queries, pack_0, pack_1)
    received = [sends[0]] + [
        lax.ppermute(sends[turn], "tp", [(at, at ^ turn) for at in range(tp_count)])
        for turn in range(1, tp_count)
    ]
    soft_mix = pl.pallas_call(
        merge_kernel,
        out_shape=jax.ShapeDtypeStruct((steps, slots, heads * LANES), jnp.bfloat16),
        in_specs=[whole()] * tp_count,
        out_specs=whole(),
        scratch_shapes=[line],
        compiler_params=params,
        cost_estimate=cost(1 << 20, 1 << 18, 1 << 10),
        name="merge",
    )(*received)

    distances = [jnp.where(move_slot[0] == slot, move_dist[0], move_dist[1]) for slot in range(slots)]
    landed_0 = migrated(pack_0, distances[0])
    landed_1 = migrated(pack_1, distances[1])

    keys, values, states, table, lengths = pl.pallas_call(
        functools.partial(unpack_kernel, steps),
        out_shape=(
            jax.ShapeDtypeStruct(key_cache.shape, jnp.bfloat16),
            jax.ShapeDtypeStruct(value_cache.shape, jnp.bfloat16),
            jax.ShapeDtypeStruct(light_state.shape, jnp.float32),
            jax.ShapeDtypeStruct(page_table.shape, jnp.int32),
            jax.ShapeDtypeStruct(context.shape, jnp.int32),
        ),
        in_specs=[whole()] * 2,
        out_specs=(whole(), whole(), whole(), whole(), scalars()),
        compiler_params=params,
        cost_estimate=cost(1 << 20, 6 << 20),
        name="unpack",
    )(landed_0, landed_1)
    return soft_mix, linear_mix, keys, values, states, table, lengths


def solution(mesh):
    placed = (
        P(None, "grp", None),
        P(None, "grp", None),
        P(None, "grp", None),
        P("grp", "tp", None, None, None),
        P("grp", "tp", None, None, None),
        P("grp", None),
        P("grp"),
        P(None, "grp", "tp"),
        P(None, "grp", "tp"),
        P(None, "grp", "tp"),
        P("grp", "tp", None, None),
        P("tp"),
        P(),
        P(),
    )
    return jax.shard_map(
        per_device,
        mesh=mesh,
        in_specs=placed,
        out_specs=(
            P(None, "grp", "tp"),
            P(None, "grp", "tp"),
            P("grp", "tp", None, None, None),
            P("grp", "tp", None, None, None),
            P("grp", "tp", None, None),
            P("grp", None),
            P("grp"),
        ),
        check_vma=False,
    )
```

```python
import functools

import jax
import jax.numpy as jnp
from jax import lax
from jax.experimental import pallas as pl
from jax.experimental.pallas import tpu as pltpu
from jax.sharding import PartitionSpec as P

MASKED_SCORE = -1e30
LANES = 128
META_ROWS = 16
DIMS0 = (((0,), (0,)), ((), ()))
DIMS1 = (((1,), (1,)), ((), ()))


def blocked(array):
    rank = len(array.shape)
    return pl.BlockSpec(array.shape, lambda i: (0,) * rank)


def scalars():
    return pl.BlockSpec(memory_space=pltpu.SMEM)


def cost(flops, moved, exps=0):
    return pl.CostEstimate(flops=flops, bytes_accessed=moved, transcendentals=exps)


def joined_rows(ref):
    value = ref[...].astype(jnp.float32)
    return jnp.concatenate([value[step] for step in range(value.shape[0])], axis=0)


def distance_of(slot, move_dist, move_slot):
    return jnp.where(move_slot[0] == slot, move_dist[0], move_dist[1])


def pieces(first, count, chunk):
    for at in range(first, first + count, 16):
        yield at - first, at // chunk, at % chunk


def rows_at(row):
    return pl.ds(pl.multiple_of(row, 16), 16)


def new_line(fresh, step, slot):
    value = fresh[step].astype(jnp.float32)
    return jnp.where(slot == 0, value[0:1], value[1:2])


def pack_kernel(
    table, context, decay, new_keys, new_values, key_cache, value_cache, light_k, light_v, state,
    send, rows_k, rows_v,
):
    slot = pl.program_id(0)
    steps, slots, width = new_keys.shape
    per_slot, page_len = key_cache.shape[2:4]
    heads = state.shape[1]
    kv_rows = per_slot * page_len
    kv_heads = width // LANES
    kv_all = 2 * kv_heads * kv_rows
    chunk = (send.shape[1] - META_ROWS) // slots
    begin = slot * chunk
    tp_rank, tp_count = lax.axis_index("tp"), lax.axis_size("tp")
    halves = ((new_keys, key_cache, 0), (new_values, value_cache, kv_heads * kv_rows))

    for _, cache, first in halves:
        for head in range(kv_heads):
            over = slice(head * LANES, (head + 1) * LANES)
            for at, place, here in pieces(first + head * kv_rows, kv_rows, chunk):
                page, row = divmod(at, page_len)
                send[place, rows_at(begin + here), :] = cache[0, 0, page, row : row + 16, over]
    for step in range(steps):
        place = context[slot] + step
        logical = place // page_len

        @pl.when(logical % tp_count == tp_rank)
        def _():
            row = (table[slot, logical] - slot * per_slot) * page_len + place % page_len
            base = row // 16 * 16
            hit = lax.broadcasted_iota(jnp.int32, (16, LANES), 0) == row - base
            for fresh, _, first in halves:
                line = new_line(fresh, step, slot)
                for head in range(kv_heads):
                    at = first + head * kv_rows + base
                    here = rows_at(begin + at % chunk)
                    old = send[at // chunk, here, :].astype(jnp.float32)
                    new = line[:, head * LANES : (head + 1) * LANES]
                    send[at // chunk, here, :] = jnp.where(hit, new, old).astype(jnp.bfloat16)

    @pl.when(slot == 0)
    def _():
        rows_k[...] = joined_rows(light_k)
        rows_v[...] = joined_rows(light_v)
        line = lax.broadcasted_iota(jnp.int32, (META_ROWS, LANES), 0)
        lane = lax.broadcasted_iota(jnp.int32, (META_ROWS, LANES), 1)
        numbers = jnp.zeros((META_ROWS, LANES), jnp.int32)
        for owner in range(slots):
            entries = [table[owner, logical] for logical in range(table.shape[1])]
            entries += [context[owner] // 256, context[owner] % 256]
            for index, entry in enumerate(entries):
                numbers = jnp.where((line == owner) & (lane == index), entry, numbers)
        numbers = numbers.astype(jnp.float32).astype(jnp.bfloat16)
        for place in range(send.shape[0]):
            send[place, slots * chunk :, :] = numbers

    row = lax.broadcasted_iota(jnp.int32, (steps * slots, LANES), 0)
    age = (steps - 1 - row // slots).astype(jnp.float32)
    mine = row % slots == slot
    for head in range(heads):
        lanes = slice(head * LANES, (head + 1) * LANES)
        rate = decay[head]
        aged = jnp.where(mine, rows_k[:, lanes] * jnp.exp(-age * rate), 0.0)
        added = lax.dot_general(
            aged.astype(jnp.bfloat16),
            rows_v[:, lanes].astype(jnp.bfloat16),
            DIMS0,
            preferred_element_type=jnp.float32,
        )
        fade = jnp.exp(jnp.full((1, LANES), -float(steps), jnp.float32) * rate)
        final = (state[0, head] * fade + added).astype(jnp.bfloat16)
        for at, place, here in pieces(kv_all + head * LANES, LANES, chunk):
            send[place, rows_at(begin + here), :] = final[at : at + 16]


def linear_kernel(
    decay, light_q, light_k, light_v, state, linear_mix, rows_q, rows_k, rows_v, rows_out
):
    slots, heads = state.shape[:2]
    steps = light_q.shape[0]
    rows_q[...] = joined_rows(light_q)
    rows_k[...] = joined_rows(light_k)
    rows_v[...] = joined_rows(light_v)
    rows = steps * slots
    row = lax.broadcasted_iota(jnp.int32, (rows, LANES), 0)
    step_of = (row // slots).astype(jnp.float32)
    first = row % slots == 0
    pair_row = lax.broadcasted_iota(jnp.int32, (rows, rows), 0)
    pair_col = lax.broadcasted_iota(jnp.int32, (rows, rows), 1)
    gap = pair_row // slots - pair_col // slots
    counted = (pair_row % slots == pair_col % slots) & (gap >= 0)
    gap = jnp.maximum(gap, 0).astype(jnp.float32)
    for head in range(heads):
        lanes = slice(head * LANES, (head + 1) * LANES)
        rate = decay[head]
        q16, k16, v16 = (part[:, lanes].astype(jnp.bfloat16) for part in (rows_q, rows_k, rows_v))
        both = [state[slot, head].astype(jnp.bfloat16) for slot in range(slots)]
        base = jnp.dot(q16, jnp.concatenate(both, axis=1), preferred_element_type=jnp.float32)
        base = jnp.where(first, base[:, :LANES], base[:, LANES:])
        base = base * jnp.exp(-(step_of + 1.0) * rate)
        match = lax.dot_general(q16, k16, DIMS1, preferred_element_type=jnp.float32)
        match = jnp.where(counted, match * jnp.exp(-gap * rate), 0.0)
        recent = jnp.dot(match.astype(jnp.bfloat16), v16, preferred_element_type=jnp.float32)
        rows_out[:, lanes] = base + recent
    for step in range(steps):
        linear_mix[step] = rows_out[step * slots : (step + 1) * slots, :].astype(jnp.bfloat16)


def thirds(value):
    high = value.astype(jnp.bfloat16)
    rest = value - high.astype(jnp.float32)
    middle = rest.astype(jnp.bfloat16)
    low = (rest - middle.astype(jnp.float32)).astype(jnp.bfloat16)
    return [part.astype(jnp.float32) for part in (high, middle, low)]


def attend_kernel(
    table, context, queries, new_keys, new_values, key_cache, value_cache, *rest
):
    *sends, pack_0, pack_1, rows_q = rest
    steps, slots, width = new_keys.shape
    page_len = key_cache.shape[3]
    per_slot = key_cache.shape[2] // slots
    kv_rows = per_slot * page_len
    kv_heads = width // LANES
    share = queries.shape[2] // width
    rows = steps * slots
    tp_rank, tp_count = lax.axis_index("tp"), lax.axis_size("tp")
    packs = (pack_0, pack_1)
    halves = ((new_keys, key_cache, 0), (new_values, value_cache, kv_heads * kv_rows))

    for slot in range(slots):
        pack = packs[slot]
        for _, cache, first in halves:
            for page in range(per_slot):
                for head in range(kv_heads):
                    at = first + head * kv_rows + page * page_len
                    over = slice(head * LANES, (head + 1) * LANES)
                    pack[at : at + page_len, :] = cache[0, 0, slot * per_slot + page, :, over]
        for step in range(steps):
            place = context[slot] + step
            logical = place // page_len

            @pl.when(logical % tp_count == tp_rank)
            def _():
                row = (table[slot, logical] - slot * per_slot) * page_len + place % page_len
                base = row // 16 * 16
                hit = lax.broadcasted_iota(jnp.int32, (16, LANES), 0) == row - base
                for fresh, _, first in halves:
                    line = new_line(fresh, step, slot)
                    for head in range(kv_heads):
                        here = pl.ds(pl.multiple_of(first + head * kv_rows + base, 16), 16)
                        old = pack[here, :].astype(jnp.float32)
                        new = line[:, head * LANES : (head + 1) * LANES]
                        pack[here, :] = jnp.where(hit, new, old).astype(jnp.bfloat16)

    rows_q[...] = joined_rows(queries)
    count = share * rows
    row = lax.broadcasted_iota(jnp.int32, (count, kv_rows), 0) % rows
    column = lax.broadcasted_iota(jnp.int32, (count, kv_rows), 1)
    limits = []
    for slot in range(slots):
        base = jnp.zeros((count, kv_rows), jnp.int32)
        for page in range(per_slot):
            number = slot * per_slot + page
            logical = 0
            for turn in range(per_slot):
                guess = turn * tp_count + tp_rank
                logical = logical + jnp.where(table[slot, guess] == number, guess, 0)
            base = jnp.where(column // page_len == page, logical * page_len, base)
        limits.append(context[slot] + row // slots - base - column % page_len)
    first = row % slots == 0
    visible = jnp.where(first, limits[0], limits[1]) >= 0
    first_out = first[:, :LANES]
    lane = lax.broadcasted_iota(jnp.int32, (count, LANES), 1)
    scale = float(LANES) ** -0.5
    per_part = kv_heads // tp_count
    for turn in range(tp_count):
        target = jnp.bitwise_xor(tp_rank, turn)
        for half in range(per_part):
            head = target * per_part + half
            query = jnp.concatenate(
                [
                    rows_q[:, pl.ds(pl.multiple_of((head * share + one) * LANES, LANES), LANES)]
                    for one in range(share)
                ],
                axis=0,
            ).astype(jnp.bfloat16)
            key_at = pl.ds(pl.multiple_of(head * kv_rows, 16), kv_rows)
            value_at = pl.ds(pl.multiple_of((kv_heads + head) * kv_rows, 16), kv_rows)
            scores = [
                lax.dot_general(query, pack[key_at, :], DIMS1, preferred_element_type=jnp.float32)
                for pack in packs
            ]
            scores = jnp.where(visible, jnp.where(first, *scores) * scale, MASKED_SCORE)
            top = jnp.max(scores, axis=-1, keepdims=True)
            weights = jnp.where(visible, jnp.exp(scores - top), 0.0)
            total = jnp.sum(weights, axis=-1, keepdims=True)
            weights = weights.astype(jnp.bfloat16)
            mixed = [
                jnp.dot(weights, pack[value_at, :], preferred_element_type=jnp.float32)
                for pack in packs
            ]
            at = slice(half * count, (half + 1) * count)
            sends[turn][at, :LANES] = jnp.where(first_out, *mixed).astype(jnp.bfloat16)
            extra = jnp.zeros((count, LANES), jnp.float32)
            for index, part in enumerate(thirds(top) + thirds(total)):
                extra = jnp.where(lane == index, part, extra)
            sends[turn][at, LANES:] = extra.astype(jnp.bfloat16)


def merge_kernel(*refs):
    parts, soft_mix, rows_out = refs[:-2], refs[-2], refs[-1]
    steps, slots, width = soft_mix.shape
    rows = steps * slots
    tops, totals = [], []
    for part in parts:
        extra = part[:, LANES:].astype(jnp.float32)
        tops.append(extra[:, 0:1] + extra[:, 1:2] + extra[:, 2:3])
        totals.append(extra[:, 3:4] + extra[:, 4:5] + extra[:, 5:6])
    peak = functools.reduce(jnp.maximum, tops)
    scales = [jnp.exp(top - peak) for top in tops]
    total = sum(total * scale for total, scale in zip(totals, scales))
    mixed = sum(part[:, :LANES].astype(jnp.float32) * scale for part, scale in zip(parts, scales))
    mixed = mixed / total
    for one in range(width // LANES):
        rows_out[:, one * LANES : (one + 1) * LANES] = mixed[one * rows : (one + 1) * rows]
    for step in range(steps):
        soft_mix[step] = rows_out[step * slots : (step + 1) * slots, :].astype(jnp.bfloat16)


def roll_kernel(slots, move_dist, move_slot, source, target):
    count = source.shape[0]
    chunk = target.shape[1] // slots
    for slot in range(slots):
        here = slice(slot * chunk, (slot + 1) * chunk)
        distance = distance_of(slot, move_dist, move_slot)

        def step(at, _):
            target[lax.rem(at + distance, count), here, :] = source[at, here, :]
            return 0

        lax.fori_loop(0, count, step, 0, unroll=4)


def unpack_kernel(
    steps, move_dist, move_slot, metas, landed, keys, values, states, table, lengths
):
    slot = pl.program_id(0)
    heads = states.shape[1]
    per_slot, page_len, width = keys.shape[2:]
    kv_rows = per_slot * page_len
    kv_heads = width // LANES
    entries = table.shape[1]
    group, count = lax.axis_index("grp"), lax.axis_size("grp")
    chunk = landed.shape[1]
    for pages, first in ((keys, 0), (values, kv_heads * kv_rows)):
        for head in range(kv_heads):
            over = slice(head * LANES, (head + 1) * LANES)
            for at, place, here in pieces(first + head * kv_rows, kv_rows, chunk):
                page, row = divmod(at, page_len)
                pages[0, 0, page, row : row + 16, over] = landed[place, here : here + 16, :]
    for head in range(heads):
        first = 2 * kv_heads * kv_rows + head * LANES
        for at, place, here in pieces(first, LANES, chunk):
            states[0, head, at : at + 16, :] = landed[place, here : here + 16, :].astype(jnp.float32)
    source = lax.rem(group - distance_of(slot, move_dist, move_slot) + count, count)
    meta = metas[source].astype(jnp.float32)
    meta = jnp.where(slot == 0, meta[0:1], meta[1:2])
    row = lax.broadcasted_iota(jnp.int32, table.shape, 0)
    table[...] = jnp.where(row == slot, meta[:, :entries].astype(jnp.int32), table[...])
    lane = lax.broadcasted_iota(jnp.int32, meta.shape, 1)
    weight = jnp.where(lane == entries, 256.0, jnp.where(lane == entries + 1, 1.0, 0.0))
    length = jnp.sum(meta * weight)
    lengths[slot] = length.astype(jnp.int32) + steps


def exchanged(value):
    return lax.all_to_all(value, "grp", 0, 0, tiled=True)


def by_slot(array, axis, slots):
    shape = tuple(size // slots if at == axis else size for at, size in enumerate(array.shape))
    return pl.BlockSpec(shape, lambda i: tuple(i if at == axis else 0 for at in range(len(shape))))


def called(kernel, out_shape, args, in_specs, out_specs, estimate, name, scratch=(), grid=1, vmem=32):
    return pl.pallas_call(
        kernel,
        grid=(grid,),
        out_shape=out_shape,
        in_specs=in_specs,
        out_specs=out_specs,
        scratch_shapes=list(scratch),
        compiler_params=pltpu.CompilerParams(vmem_limit_bytes=vmem * 1024 * 1024),
        cost_estimate=estimate,
        name=name,
    )(*args)


def per_device(
    queries,
    new_keys,
    new_values,
    key_cache,
    value_cache,
    page_table,
    context,
    light_q,
    light_k,
    light_v,
    light_state,
    decay_rate,
    move_dist,
    move_slot,
):
    steps, slots, width = new_keys.shape
    page_len = key_cache.shape[3]
    per_slot = key_cache.shape[2] // slots
    heads = light_state.shape[1]
    kv_all = 2 * per_slot * page_len * width // LANES
    tp_count, groups = lax.axis_size("tp"), lax.axis_size("grp")
    rows = steps * slots
    shape = jax.ShapeDtypeStruct
    line = pltpu.VMEM((rows, heads * LANES), jnp.float32)
    chunk = (kv_all + heads * LANES) // groups
    send_all = shape((groups, slots * chunk, LANES), jnp.bfloat16)

    first_all = shape((groups, slots * chunk + META_ROWS, LANES), jnp.bfloat16)

    send = called(
        pack_kernel,
        first_all,
        (
            page_table, context, decay_rate, new_keys, new_values, key_cache, value_cache,
            light_k, light_v, light_state,
        ),
        [scalars()] * 3
        + [blocked(new_keys), blocked(new_values)]
        + [by_slot(key_cache, 2, slots), by_slot(value_cache, 2, slots)]
        + [blocked(light_k), blocked(light_v), by_slot(light_state, 0, slots)],
        blocked(first_all),
        cost(1 << 24, 7 << 20),
        "pack",
        [line] * 2,
        slots,
        60,
    )
    spread = exchanged(send)

    linear_mix = called(
        linear_kernel,
        shape(light_q.shape, jnp.bfloat16),
        (decay_rate, light_q, light_k, light_v, light_state),
        [scalars()] + [blocked(arg) for arg in (light_q, light_k, light_v, light_state)],
        blocked(light_q),
        cost(1 << 24, 3 << 20),
        "linear",
        [line] * 4,
    )

    send_rows = rows * queries.shape[2] // LANES // tp_count
    send_shape = shape((send_rows, 2 * LANES), jnp.bfloat16)
    attended = (queries, new_keys, new_values, key_cache, value_cache)
    sends = called(
        attend_kernel,
        (send_shape,) * tp_count,
        (page_table, context, *attended),
        [scalars()] * 2 + [blocked(arg) for arg in attended],
        (blocked(send_shape),) * tp_count,
        cost(1 << 28, 2 << 20, 1 << 18),
        "attend",
        [pltpu.VMEM((kv_all, LANES), jnp.bfloat16)] * slots
        + [pltpu.VMEM((rows, queries.shape[2]), jnp.float32)],
    )
    received = [sends[0]] + [
        lax.ppermute(sends[turn], "tp", [(at, at ^ turn) for at in range(tp_count)])
        for turn in range(1, tp_count)
    ]

    turned = called(
        functools.partial(roll_kernel, slots),
        send_all,
        (move_dist, move_slot, spread),
        [scalars()] * 2 + [blocked(first_all)],
        blocked(send_all),
        cost(1 << 10, 5 << 20),
        "roll",
    )
    landed = exchanged(turned)

    mixed = shape((steps, slots, heads * LANES), jnp.bfloat16)
    soft_mix = called(
        merge_kernel,
        mixed,
        tuple(received),
        [blocked(send_shape)] * tp_count,
        blocked(mixed),
        cost(1 << 20, 1 << 18, 1 << 10),
        "merge",
        [line],
    )
    outs = (
        shape(key_cache.shape, jnp.bfloat16),
        shape(value_cache.shape, jnp.bfloat16),
        shape(light_state.shape, jnp.float32),
        shape(page_table.shape, jnp.int32),
        shape(context.shape, jnp.int32),
    )
    metas = pl.BlockSpec((groups, META_ROWS, LANES), lambda i: (0, slots * chunk // META_ROWS, 0))
    keys, values, states, table, lengths = called(
        functools.partial(unpack_kernel, steps),
        outs,
        (move_dist, move_slot, spread, landed),
        [scalars()] * 2 + [metas, by_slot(send_all, 1, slots)],
        (
            by_slot(outs[0], 2, slots), by_slot(outs[1], 2, slots), by_slot(outs[2], 0, slots),
            blocked(outs[3]), scalars(),
        ),
        cost(1 << 20, 6 << 20),
        "unpack",
        (),
        slots,
    )
    return soft_mix, linear_mix, keys, values, states, table, lengths


def solution(mesh):
    placed = (
        P(None, "grp", None),
        P(None, "grp", None),
        P(None, "grp", None),
        P("grp", "tp", None, None, None),
        P("grp", "tp", None, None, None),
        P("grp", None),
        P("grp"),
        P(None, "grp", "tp"),
        P(None, "grp", "tp"),
        P(None, "grp", "tp"),
        P("grp", "tp", None, None),
        P("tp"),
        P(),
        P(),
    )
    return jax.shard_map(
        per_device,
        mesh=mesh,
        in_specs=placed,
        out_specs=(
            P(None, "grp", "tp"),
            P(None, "grp", "tp"),
            P("grp", "tp", None, None, None),
            P("grp", "tp", None, None, None),
            P("grp", "tp", None, None),
            P("grp", None),
            P("grp"),
        ),
        check_vma=False,
    )
```

```python
import functools

import jax
import jax.numpy as jnp
from jax import lax
from jax.experimental import pallas as pl
from jax.experimental.pallas import tpu as pltpu
from jax.sharding import PartitionSpec as P

MASKED_SCORE = -1e30
LANES = 128
META_ROWS = 8
ROLL_PARTS = 4
DIMS0 = (((0,), (0,)), ((), ()))
DIMS1 = (((1,), (1,)), ((), ()))


def blocked(array):
    rank = len(array.shape)
    return pl.BlockSpec(array.shape, lambda i: (0,) * rank)


def scalars():
    return pl.BlockSpec(memory_space=pltpu.SMEM)


def cost(flops, moved, exps=0):
    return pl.CostEstimate(flops=flops, bytes_accessed=moved, transcendentals=exps)


def joined_rows(ref):
    value = ref[...].astype(jnp.float32)
    return jnp.concatenate([value[step] for step in range(value.shape[0])], axis=0)


def distance_of(slot, move_dist, move_slot):
    return jnp.where(move_slot[0] == slot, move_dist[0], move_dist[1])


def pieces(first, count, chunk):
    for at in range(first, first + count, 16):
        yield at - first, at // chunk, at % chunk


def rows_at(row):
    return pl.ds(pl.multiple_of(row, 16), 16)


def new_line(fresh, step, slot):
    value = fresh[step].astype(jnp.float32)
    return jnp.where(slot == 0, value[0:1], value[1:2])


def pack_kernel(
    table, context, decay, new_keys, new_values, key_cache, value_cache, light_k, light_v, state,
    send, rows_k, rows_v,
):
    slot = pl.program_id(0)
    steps, slots, width = new_keys.shape
    per_slot, page_len = key_cache.shape[2:4]
    heads = state.shape[1]
    kv_rows = per_slot * page_len
    kv_heads = width // LANES
    kv_all = 2 * kv_heads * kv_rows
    chunk = (send.shape[1] - META_ROWS) // slots
    begin = slot * chunk
    tp_rank, tp_count = lax.axis_index("tp"), lax.axis_size("tp")
    halves = ((new_keys, key_cache, 0), (new_values, value_cache, kv_heads * kv_rows))

    for _, cache, first in halves:
        for head in range(kv_heads):
            over = slice(head * LANES, (head + 1) * LANES)
            for at, place, here in pieces(first + head * kv_rows, kv_rows, chunk):
                page, row = divmod(at, page_len)
                send[place, rows_at(begin + here), :] = cache[0, 0, page, row : row + 16, over]
    for step in range(steps):
        place = context[slot] + step
        logical = place // page_len

        @pl.when(logical % tp_count == tp_rank)
        def _():
            row = (table[slot, logical] - slot * per_slot) * page_len + place % page_len
            base = row // 16 * 16
            hit = lax.broadcasted_iota(jnp.int32, (16, LANES), 0) == row - base
            for fresh, _, first in halves:
                line = new_line(fresh, step, slot)
                for head in range(kv_heads):
                    at = first + head * kv_rows + base
                    here = rows_at(begin + at % chunk)
                    old = send[at // chunk, here, :].astype(jnp.float32)
                    new = line[:, head * LANES : (head + 1) * LANES]
                    send[at // chunk, here, :] = jnp.where(hit, new, old).astype(jnp.bfloat16)

    @pl.when(slot == 0)
    def _():
        rows_k[...] = joined_rows(light_k)
        rows_v[...] = joined_rows(light_v)
        line = lax.broadcasted_iota(jnp.int32, (META_ROWS, LANES), 0)
        lane = lax.broadcasted_iota(jnp.int32, (META_ROWS, LANES), 1)
        numbers = jnp.zeros((META_ROWS, LANES), jnp.int32)
        for owner in range(slots):
            entries = [table[owner, logical] for logical in range(table.shape[1])]
            entries += [context[owner] // 256, context[owner] % 256]
            for index, entry in enumerate(entries):
                numbers = jnp.where((line == owner) & (lane == index), entry, numbers)
        numbers = numbers.astype(jnp.float32).astype(jnp.bfloat16)
        for place in range(send.shape[0]):
            send[place, slots * chunk :, :] = numbers

    row = lax.broadcasted_iota(jnp.int32, (steps * slots, LANES), 0)
    age = (steps - 1 - row // slots).astype(jnp.float32)
    mine = row % slots == slot
    for head in range(heads):
        lanes = slice(head * LANES, (head + 1) * LANES)
        rate = decay[head]
        aged = jnp.where(mine, rows_k[:, lanes] * jnp.exp(-age * rate), 0.0)
        added = lax.dot_general(
            aged.astype(jnp.bfloat16),
            rows_v[:, lanes].astype(jnp.bfloat16),
            DIMS0,
            preferred_element_type=jnp.float32,
        )
        fade = jnp.exp(jnp.full((1, LANES), -float(steps), jnp.float32) * rate)
        final = (state[0, head] * fade + added).astype(jnp.bfloat16)
        for at, place, here in pieces(kv_all + head * LANES, LANES, chunk):
            send[place, rows_at(begin + here), :] = final[at : at + 16]


def linear_kernel(
    decay, light_q, light_k, light_v, state, linear_mix, rows_q, rows_k, rows_v, rows_out
):
    slots, heads = state.shape[:2]
    steps = light_q.shape[0]
    rows_q[...] = joined_rows(light_q)
    rows_k[...] = joined_rows(light_k)
    rows_v[...] = joined_rows(light_v)
    rows = steps * slots
    row = lax.broadcasted_iota(jnp.int32, (rows, LANES), 0)
    step_of = (row // slots).astype(jnp.float32)
    first = row % slots == 0
    pair_row = lax.broadcasted_iota(jnp.int32, (rows, rows), 0)
    pair_col = lax.broadcasted_iota(jnp.int32, (rows, rows), 1)
    gap = pair_row // slots - pair_col // slots
    counted = (pair_row % slots == pair_col % slots) & (gap >= 0)
    gap = jnp.maximum(gap, 0).astype(jnp.float32)
    for head in range(heads):
        lanes = slice(head * LANES, (head + 1) * LANES)
        rate = decay[head]
        q16, k16, v16 = (part[:, lanes].astype(jnp.bfloat16) for part in (rows_q, rows_k, rows_v))
        both = [state[slot, head].astype(jnp.bfloat16) for slot in range(slots)]
        base = jnp.dot(q16, jnp.concatenate(both, axis=1), preferred_element_type=jnp.float32)
        base = jnp.where(first, base[:, :LANES], base[:, LANES:])
        base = base * jnp.exp(-(step_of + 1.0) * rate)
        match = lax.dot_general(q16, k16, DIMS1, preferred_element_type=jnp.float32)
        match = jnp.where(counted, match * jnp.exp(-gap * rate), 0.0)
        recent = jnp.dot(match.astype(jnp.bfloat16), v16, preferred_element_type=jnp.float32)
        rows_out[:, lanes] = base + recent
    for step in range(steps):
        linear_mix[step] = rows_out[step * slots : (step + 1) * slots, :].astype(jnp.bfloat16)


def thirds(value):
    high = value.astype(jnp.bfloat16)
    rest = value - high.astype(jnp.float32)
    middle = rest.astype(jnp.bfloat16)
    low = (rest - middle.astype(jnp.float32)).astype(jnp.bfloat16)
    return [part.astype(jnp.float32) for part in (high, middle, low)]


def attend_kernel(
    table, context, queries, new_keys, new_values, key_cache, value_cache, *rest
):
    *sends, pack_0, pack_1, rows_q = rest
    steps, slots, width = new_keys.shape
    page_len = key_cache.shape[3]
    per_slot = key_cache.shape[2] // slots
    kv_rows = per_slot * page_len
    kv_heads = width // LANES
    share = queries.shape[2] // width
    rows = steps * slots
    tp_rank, tp_count = lax.axis_index("tp"), lax.axis_size("tp")
    packs = (pack_0, pack_1)
    halves = ((new_keys, key_cache, 0), (new_values, value_cache, kv_heads * kv_rows))

    for slot in range(slots):
        pack = packs[slot]
        for _, cache, first in halves:
            for page in range(per_slot):
                for head in range(kv_heads):
                    at = first + head * kv_rows + page * page_len
                    over = slice(head * LANES, (head + 1) * LANES)
                    pack[at : at + page_len, :] = cache[0, 0, slot * per_slot + page, :, over]
        for step in range(steps):
            place = context[slot] + step
            logical = place // page_len

            @pl.when(logical % tp_count == tp_rank)
            def _():
                row = (table[slot, logical] - slot * per_slot) * page_len + place % page_len
                base = row // 16 * 16
                hit = lax.broadcasted_iota(jnp.int32, (16, LANES), 0) == row - base
                for fresh, _, first in halves:
                    line = new_line(fresh, step, slot)
                    for head in range(kv_heads):
                        here = pl.ds(pl.multiple_of(first + head * kv_rows + base, 16), 16)
                        old = pack[here, :].astype(jnp.float32)
                        new = line[:, head * LANES : (head + 1) * LANES]
                        pack[here, :] = jnp.where(hit, new, old).astype(jnp.bfloat16)

    rows_q[...] = joined_rows(queries)
    count = share * rows
    row = lax.broadcasted_iota(jnp.int32, (count, kv_rows), 0) % rows
    column = lax.broadcasted_iota(jnp.int32, (count, kv_rows), 1)
    limits = []
    for slot in range(slots):
        base = jnp.zeros((count, kv_rows), jnp.int32)
        for page in range(per_slot):
            number = slot * per_slot + page
            logical = 0
            for turn in range(per_slot):
                guess = turn * tp_count + tp_rank
                logical = logical + jnp.where(table[slot, guess] == number, guess, 0)
            base = jnp.where(column // page_len == page, logical * page_len, base)
        limits.append(context[slot] + row // slots - base - column % page_len)
    first = row % slots == 0
    visible = jnp.where(first, limits[0], limits[1]) >= 0
    first_out = first[:, :LANES]
    lane = lax.broadcasted_iota(jnp.int32, (count, LANES), 1)
    scale = float(LANES) ** -0.5
    per_part = kv_heads // tp_count
    for turn in range(tp_count):
        target = jnp.bitwise_xor(tp_rank, turn)
        for half in range(per_part):
            head = target * per_part + half
            query = jnp.concatenate(
                [
                    rows_q[:, pl.ds(pl.multiple_of((head * share + one) * LANES, LANES), LANES)]
                    for one in range(share)
                ],
                axis=0,
            ).astype(jnp.bfloat16)
            key_at = pl.ds(pl.multiple_of(head * kv_rows, 16), kv_rows)
            value_at = pl.ds(pl.multiple_of((kv_heads + head) * kv_rows, 16), kv_rows)
            scores = [
                lax.dot_general(query, pack[key_at, :], DIMS1, preferred_element_type=jnp.float32)
                for pack in packs
            ]
            scores = jnp.where(visible, jnp.where(first, *scores) * scale, MASKED_SCORE)
            top = jnp.max(scores, axis=-1, keepdims=True)
            weights = jnp.where(visible, jnp.exp(scores - top), 0.0)
            total = jnp.sum(weights, axis=-1, keepdims=True)
            weights = weights.astype(jnp.bfloat16)
            mixed = [
                jnp.dot(weights, pack[value_at, :], preferred_element_type=jnp.float32)
                for pack in packs
            ]
            at = slice(half * count, (half + 1) * count)
            sends[turn][at, :LANES] = jnp.where(first_out, *mixed).astype(jnp.bfloat16)
            extra = jnp.zeros((count, LANES), jnp.float32)
            for index, part in enumerate(thirds(top) + thirds(total)):
                extra = jnp.where(lane == index, part, extra)
            sends[turn][at, LANES:] = extra.astype(jnp.bfloat16)


def merge_kernel(*refs):
    parts, soft_mix, rows_out = refs[:-2], refs[-2], refs[-1]
    steps, slots, width = soft_mix.shape
    rows = steps * slots
    tops, totals = [], []
    for part in parts:
        extra = part[:, LANES:].astype(jnp.float32)
        tops.append(extra[:, 0:1] + extra[:, 1:2] + extra[:, 2:3])
        totals.append(extra[:, 3:4] + extra[:, 4:5] + extra[:, 5:6])
    peak = functools.reduce(jnp.maximum, tops)
    scales = [jnp.exp(top - peak) for top in tops]
    total = sum(total * scale for total, scale in zip(totals, scales))
    mixed = sum(part[:, :LANES].astype(jnp.float32) * scale for part, scale in zip(parts, scales))
    mixed = mixed / total
    for one in range(width // LANES):
        rows_out[:, one * LANES : (one + 1) * LANES] = mixed[one * rows : (one + 1) * rows]
    for step in range(steps):
        soft_mix[step] = rows_out[step * slots : (step + 1) * slots, :].astype(jnp.bfloat16)


def roll_kernel(slots, move_dist, move_slot, source, target, metas):
    count = source.shape[0]
    part = target.shape[0]
    chunk = target.shape[1] // slots
    begin = pl.program_id(0) * part
    group = lax.axis_index("grp")
    for slot in range(slots):
        here = slice(slot * chunk, (slot + 1) * chunk)
        distance = distance_of(slot, move_dist, move_slot)
        for at in range(part):
            origin = lax.rem(begin + at - distance + count, count)
            target[at, here, :] = source[origin, here, :]
        sender = lax.rem(group - distance + count, count)
        lines = source[sender, slots * chunk :, :].astype(jnp.float32)
        metas[slot : slot + 1, :] = lines[slot : slot + 1]


def unpack_kernel(
    steps, metas, landed, keys, values, states, table, lengths
):
    slot = pl.program_id(0)
    heads = states.shape[1]
    per_slot, page_len, width = keys.shape[2:]
    kv_rows = per_slot * page_len
    kv_heads = width // LANES
    entries = table.shape[1]
    chunk = landed.shape[1]
    for pages, first in ((keys, 0), (values, kv_heads * kv_rows)):
        for head in range(kv_heads):
            over = slice(head * LANES, (head + 1) * LANES)
            for at, place, here in pieces(first + head * kv_rows, kv_rows, chunk):
                page, row = divmod(at, page_len)
                pages[0, 0, page, row : row + 16, over] = landed[place, here : here + 16, :]
    for head in range(heads):
        first = 2 * kv_heads * kv_rows + head * LANES
        for at, place, here in pieces(first, LANES, chunk):
            states[0, head, at : at + 16, :] = landed[place, here : here + 16, :].astype(jnp.float32)
    meta = jnp.where(slot == 0, metas[0:1], metas[1:2])
    row = lax.broadcasted_iota(jnp.int32, table.shape, 0)
    table[...] = jnp.where(row == slot, meta[:, :entries].astype(jnp.int32), table[...])
    lane = lax.broadcasted_iota(jnp.int32, meta.shape, 1)
    weight = jnp.where(lane == entries, 256.0, jnp.where(lane == entries + 1, 1.0, 0.0))
    length = jnp.sum(meta * weight)
    lengths[slot] = length.astype(jnp.int32) + steps


def exchanged(value):
    return lax.all_to_all(value, "grp", 0, 0, tiled=True)


def by_part(array, axis, parts):
    shape = tuple(size // parts if at == axis else size for at, size in enumerate(array.shape))
    return pl.BlockSpec(shape, lambda i: tuple(i if at == axis else 0 for at in range(len(shape))))


def called(kernel, out_shape, args, in_specs, out_specs, estimate, name, scratch=(), grid=1, vmem=32):
    return pl.pallas_call(
        kernel,
        grid=(grid,),
        out_shape=out_shape,
        in_specs=in_specs,
        out_specs=out_specs,
        scratch_shapes=list(scratch),
        compiler_params=pltpu.CompilerParams(vmem_limit_bytes=vmem * 1024 * 1024),
        cost_estimate=estimate,
        name=name,
    )(*args)


def per_device(
    queries,
    new_keys,
    new_values,
    key_cache,
    value_cache,
    page_table,
    context,
    light_q,
    light_k,
    light_v,
    light_state,
    decay_rate,
    move_dist,
    move_slot,
):
    steps, slots, width = new_keys.shape
    page_len = key_cache.shape[3]
    per_slot = key_cache.shape[2] // slots
    heads = light_state.shape[1]
    kv_all = 2 * per_slot * page_len * width // LANES
    tp_count, groups = lax.axis_size("tp"), lax.axis_size("grp")
    rows = steps * slots
    shape = jax.ShapeDtypeStruct
    line = pltpu.VMEM((rows, heads * LANES), jnp.float32)
    chunk = (kv_all + heads * LANES) // groups
    send_all = shape((groups, slots * chunk, LANES), jnp.bfloat16)

    first_all = shape((groups, slots * chunk + META_ROWS, LANES), jnp.bfloat16)

    send = called(
        pack_kernel,
        first_all,
        (
            page_table, context, decay_rate, new_keys, new_values, key_cache, value_cache,
            light_k, light_v, light_state,
        ),
        [scalars()] * 3
        + [blocked(new_keys), blocked(new_values)]
        + [by_part(key_cache, 2, slots), by_part(value_cache, 2, slots)]
        + [blocked(light_k), blocked(light_v), by_part(light_state, 0, slots)],
        blocked(first_all),
        cost(1 << 24, 7 << 20),
        "pack",
        [line] * 2,
        slots,
        60,
    )
    spread = exchanged(send)

    linear_mix = called(
        linear_kernel,
        shape(light_q.shape, jnp.bfloat16),
        (decay_rate, light_q, light_k, light_v, light_state),
        [scalars()] + [blocked(arg) for arg in (light_q, light_k, light_v, light_state)],
        blocked(light_q),
        cost(1 << 24, 3 << 20),
        "linear",
        [line] * 4,
    )

    send_rows = rows * queries.shape[2] // LANES // tp_count
    send_shape = shape((send_rows, 2 * LANES), jnp.bfloat16)
    attended = (queries, new_keys, new_values, key_cache, value_cache)
    sends = called(
        attend_kernel,
        (send_shape,) * tp_count,
        (page_table, context, *attended),
        [scalars()] * 2 + [blocked(arg) for arg in attended],
        (blocked(send_shape),) * tp_count,
        cost(1 << 28, 2 << 20, 1 << 18),
        "attend",
        [pltpu.VMEM((kv_all, LANES), jnp.bfloat16)] * slots
        + [pltpu.VMEM((rows, queries.shape[2]), jnp.float32)],
    )
    spread, *sends = lax.optimization_barrier((spread, *sends))
    received = [sends[0]] + [
        lax.ppermute(sends[turn], "tp", [(at, at ^ turn) for at in range(tp_count)])
        for turn in range(1, tp_count)
    ]

    meta_all = shape((slots, LANES), jnp.float32)
    turned, metas = called(
        functools.partial(roll_kernel, slots),
        (send_all, meta_all),
        (move_dist, move_slot, spread),
        [scalars()] * 2 + [blocked(first_all)],
        (by_part(send_all, 0, ROLL_PARTS), blocked(meta_all)),
        cost(1 << 10, 5 << 20),
        "roll",
        grid=ROLL_PARTS,
        vmem=60,
    )
    landed = exchanged(turned)

    mixed = shape((steps, slots, heads * LANES), jnp.bfloat16)
    soft_mix = called(
        merge_kernel,
        mixed,
        tuple(received),
        [blocked(send_shape)] * tp_count,
        blocked(mixed),
        cost(1 << 20, 1 << 18, 1 << 10),
        "merge",
        [line],
    )
    outs = (
        shape(key_cache.shape, jnp.bfloat16),
        shape(value_cache.shape, jnp.bfloat16),
        shape(light_state.shape, jnp.float32),
        shape(page_table.shape, jnp.int32),
        shape(context.shape, jnp.int32),
    )
    keys, values, states, table, lengths = called(
        functools.partial(unpack_kernel, steps),
        outs,
        (metas, landed),
        [blocked(meta_all), by_part(send_all, 1, slots)],
        (
            by_part(outs[0], 2, slots), by_part(outs[1], 2, slots), by_part(outs[2], 0, slots),
            blocked(outs[3]), scalars(),
        ),
        cost(1 << 20, 6 << 20),
        "unpack",
        (),
        slots,
    )
    return soft_mix, linear_mix, keys, values, states, table, lengths


def solution(mesh):
    placed = (
        P(None, "grp", None),
        P(None, "grp", None),
        P(None, "grp", None),
        P("grp", "tp", None, None, None),
        P("grp", "tp", None, None, None),
        P("grp", None),
        P("grp"),
        P(None, "grp", "tp"),
        P(None, "grp", "tp"),
        P(None, "grp", "tp"),
        P("grp", "tp", None, None),
        P("tp"),
        P(),
        P(),
    )
    return jax.shard_map(
        per_device,
        mesh=mesh,
        in_specs=placed,
        out_specs=(
            P(None, "grp", "tp"),
            P(None, "grp", "tp"),
            P("grp", "tp", None, None, None),
            P("grp", "tp", None, None, None),
            P("grp", "tp", None, None),
            P("grp", None),
            P("grp"),
        ),
        check_vma=False,
    )
```
